1024 devices in a mesh: dp: 16 (over y, core), expert: 64 (over z, x).
Axes of the slice: x: 4, y: 8, z: 16, core: 2. Of those that a mesh axis runs over, the one named last changes fastest.
Arguments:
- tokens: bfloat16 [131072, 4096], P(('dp', 'expert')), may hold values from -24 to 24
- cotangent: bfloat16 [131072, 4096], P(('dp', 'expert')), may hold values from -24 to 24
- slot_token: int32 [1024, 16], P(('dp', 'expert')), may hold values from 0 to 127, as said below
- slot_gate: int32 [1024, 16], P(('dp', 'expert')), may hold values from 0 to 1023, as said below
- gate_weight: bfloat16 [4096, 8192], P(None, 'expert'), may hold values from -0.09375 to 0.09375
- up_weight: bfloat16 [4096, 8192], P(None, 'expert'), may hold values from -0.09375 to 0.09375
- down_weight: bfloat16 [8192, 4096], P('expert'), may hold values from -0.1875 to 0.1875
Outputs:
- token_grad: bfloat16 [131072, 4096], P(('dp', 'expert'))
- gate_grad: bfloat16 [4096, 8192], P('dp', 'expert')
- up_grad: bfloat16 [4096, 8192], P('dp', 'expert')
- down_grad: bfloat16 [8192, 4096], P('expert', 'dp')
The draws below stay inside these ranges and needn't reach their ends.
Inputs may be any that keep to these rules, and one draw needn't show every extreme that they name: `slot_token`: entry f * 2 + k of row r is the token within block r in the k-th slot that expert f fills from that block; the 2 entries of one block and expert are distinct. `slot_gate`: the gate weight is the code / 1024; a code is 0 exactly in an empty slot, and the empty slots of one block and expert follow its filled ones. Each block fills 0 to 2 slots of each expert; blocks 2i and 2i + 1 of a data group together fill exactly 2 slots of each expert; some block of every data group fills all 2 of each expert, and each expert fills exactly 64 slots over the 64 blocks of one data group.
All inputs are finite; a program needn't handle non-finite values.
Results may differ from the reference program's by a relative error of at most 0.023.
Values may be sent and summed in bfloat16 or wider, within the bound.
A program may use at most 32 MiB of HBM per device.

```python
import jax
import jax.numpy as jnp
from jax import lax

D = 4096
FF = 1024
SHARDS = 8
TOK_DEV = 128
SLOT = 2
HD = 128
GROUPS = 16
GROUP = 64
SOURCES = 1024
FLIGHT = 8
TOKENS = 131072


def slot_counts(key):
    pair_count = GROUP // 2
    first_count = jax.random.randint(jax.random.fold_in(key, 11), (GROUPS, pair_count, FLIGHT), 0, SLOT + 1)
    forced_pair = jax.random.randint(jax.random.fold_in(key, 12), (GROUPS, 1, FLIGHT), 0, pair_count)
    forced_side = jax.random.randint(jax.random.fold_in(key, 13), (GROUPS, 1, FLIGHT), 0, 2) * SLOT
    position = jnp.arange(pair_count, dtype=jnp.int32)[None, :, None]
    first = jnp.where(position == forced_pair, forced_side, first_count)
    second = SLOT - first
    paired = jnp.stack((first, second), axis=2)
    return paired.reshape(SOURCES, FLIGHT).astype(jnp.int32)


def draw_slot_gate(key, part):
    counts = slot_counts(key)
    key = jax.random.fold_in(key, 2)
    gate_codes = jax.random.randint(key, (SOURCES, FLIGHT, SLOT), 1, 1024)
    filled = jnp.arange(SLOT, dtype=jnp.int32)[None, None, :] < counts[:, :, None]
    return jnp.where(filled, gate_codes, 0).reshape(SOURCES, FLIGHT * SLOT).astype(jnp.int32)


def draw_slot_token(key, part):
    key = jax.random.fold_in(key, 3)
    scores = jax.random.randint(key, (SOURCES, FLIGHT, TOK_DEV), 0, 1 << 20) * TOK_DEV + jnp.arange(TOK_DEV, dtype=jnp.int32)
    ranking = jnp.argsort(scores, axis=-1)
    return ranking[:, :, :SLOT].reshape(SOURCES, FLIGHT * SLOT).astype(jnp.int32)


def with_spikes(array, rng, source, target, shards_of, factor):
    def block_of(dim):
        return (jnp.arange(array.shape[dim]) // (array.shape[dim] // shards_of)).reshape((-1,) + (1,) * (array.ndim - 1 - dim))

    one_side = jax.random.permutation(rng, shards_of)[block_of(target)]
    other_side = (block_of(target) + shards_of // 2) % shards_of
    return jnp.where((block_of(source) == one_side) | (block_of(source) == other_side), factor * array, array)


def levels(rng, extent, split, smallest, high):
    def one(dim, shards_of):
        draws = jax.random.uniform(jax.random.fold_in(jax.random.fold_in(rng, 6), dim), (shards_of,), jnp.float32, smallest / len(split), high / len(split))
        return jnp.repeat(jnp.exp(draws), extent[dim] // shards_of).reshape((-1,) + (1,) * (len(extent) - dim - 1))

    level = one(*split[0])
    for cut in split[1:]:
        level = level * one(*cut)
    return level


def bell_draw(rng, shape, scale, limit, pieces=(), kind=jnp.bfloat16):
    entries = jax.random.normal(rng, shape, jnp.float32) * scale
    if len(pieces) > 0:
        entries = levels(rng, shape, pieces, -0.22, 0.18) * entries
    return jnp.clip(entries, min=-limit, max=limit).astype(kind)


def heavy_noise(stream_key, dims, deviation, bound, shards, heavy, kind=jnp.bfloat16):
    result = deviation * jax.random.normal(stream_key, dims, jnp.float32)
    if shards:
        result = result * levels(stream_key, dims, shards, -0.22, 0.18)
    return jnp.clip(with_spikes(result, jax.random.fold_in(stream_key, 3), *heavy), -bound, bound).astype(kind)


def setup_inputs(seed: int = 0) -> dict:
    key_list = jax.random.split(jax.random.key(seed), 8)
    tokens = heavy_noise(key_list[0], (TOKENS, D), 1.0, 24.0, ((0, 1024),), (0, 1, 1024, 6.0))
    cotangent = heavy_noise(key_list[1], (TOKENS, D), 1.0, 24.0, ((0, 1024),), (0, 1, 1024, 6.0))
    slot_token = draw_slot_token(jax.random.fold_in(key_list[7], 71), 0)
    slot_gate = draw_slot_gate(jax.random.fold_in(key_list[7], 71), 0)
    gate_weight = bell_draw(key_list[4], (D, FLIGHT * FF), D ** -0.5, 0.09375, ((1, 64),))
    up_weight = bell_draw(key_list[5], (D, FLIGHT * FF), D ** -0.5, 0.09375, ((1, 64),))
    down_weight = bell_draw(key_list[6], (FLIGHT * FF, D), FF ** -0.5, 0.1875, ((0, 64),))
    return dict(tokens=tokens, cotangent=cotangent, slot_token=slot_token, slot_gate=slot_gate, gate_weight=gate_weight, up_weight=up_weight, down_weight=down_weight)


def rounded(value):
    return lax.optimization_barrier(value.astype(jnp.bfloat16)).astype(jnp.float32)

def reference(tokens, cotangent, slot_token, slot_gate, gate_weight, up_weight, down_weight):
    slot_rows = SOURCES * SLOT
    first_axes = (((0,), (0,)), ((), ()))
    local_index = slot_token.reshape(SOURCES, FLIGHT, SLOT)
    offset = (jnp.arange(SOURCES, dtype=jnp.int32) * TOK_DEV)[:, None, None]
    chosen = jnp.transpose(local_index + offset, (1, 0, 2)).reshape(FLIGHT, slot_rows).astype(jnp.int32)
    slot_weight = jnp.transpose(slot_gate.reshape(SOURCES, FLIGHT, SLOT).astype(jnp.float32) / 1024.0, (1, 0, 2)).reshape(FLIGHT, slot_rows)
    gate_blocks = jnp.transpose(gate_weight.reshape(D, FLIGHT, FF), (1, 0, 2))
    up_blocks = jnp.transpose(up_weight.reshape(D, FLIGHT, FF), (1, 0, 2))
    down_blocks = down_weight.reshape(FLIGHT, FF, D)

    def one_expert(packed):
        picks, weights, w_gate, w_up, w_down = packed
        token_rows = tokens[picks]
        gated_rows = (weights[:, None] * cotangent[picks].astype(jnp.float32)).astype(jnp.bfloat16)
        pre_gate = jnp.dot(token_rows, w_gate, preferred_element_type=jnp.float32)
        pre_up = jnp.dot(token_rows, w_up, preferred_element_type=jnp.float32)
        sigmoid_gate = jax.nn.sigmoid(pre_gate)
        activated = pre_gate * sigmoid_gate
        hidden_act = (activated * pre_up).astype(jnp.bfloat16)
        hidden_grad = jnp.dot(gated_rows, w_down.T, preferred_element_type=jnp.float32)
        grad_gate = (hidden_grad * pre_up * sigmoid_gate * (1.0 + pre_gate * (1.0 - sigmoid_gate))).astype(jnp.bfloat16)
        grad_up = (hidden_grad * activated).astype(jnp.bfloat16)
        partial_value = jnp.zeros((slot_rows, D), jnp.float32)
        for group_index in range(SHARDS):
            low_col = group_index * HD
            high_col = low_col + HD
            piece = jnp.dot(grad_gate[:, low_col:high_col], w_gate[:, low_col:high_col].T, preferred_element_type=jnp.float32)
            piece = piece + jnp.dot(grad_up[:, low_col:high_col], w_up[:, low_col:high_col].T, preferred_element_type=jnp.float32)
            partial_value = partial_value + rounded(piece)

        def group_sum(totals, members):
            group_rows, group_gate, group_up, group_hidden, group_grads = members
            gate_part = lax.dot_general(group_rows, group_gate, first_axes, preferred_element_type=jnp.float32)
            up_part = lax.dot_general(group_rows, group_up, first_axes, preferred_element_type=jnp.float32)
            down_part = lax.dot_general(group_hidden, group_grads, first_axes, preferred_element_type=jnp.float32)
            return ((totals[0] + rounded(gate_part), totals[1] + rounded(up_part), totals[2] + rounded(down_part)), None)
        per_group = GROUP * SLOT
        members = (token_rows.reshape(GROUPS, per_group, D), grad_gate.reshape(GROUPS, per_group, FF), grad_up.reshape(GROUPS, per_group, FF), hidden_act.reshape(GROUPS, per_group, FF), gated_rows.reshape(GROUPS, per_group, D))
        start = (jnp.zeros((D, FF), jnp.float32), jnp.zeros((D, FF), jnp.float32), jnp.zeros((FF, D), jnp.float32))
        totals, unused = lax.scan(group_sum, start, members)
        return (partial_value, totals[0], totals[1], totals[2])
    partials, gate_sums, up_sums, down_sums = lax.map(one_expert, (chosen, slot_weight, gate_blocks, up_blocks, down_blocks))
    per_block = jnp.transpose(partials.reshape(FLIGHT, SOURCES, SLOT, D), (1, 0, 2, 3)).reshape(SOURCES, FLIGHT * SLOT, D)

    def block_grad(packed):
        contributions, targets = packed
        return jax.ops.segment_sum(contributions, targets, num_segments=TOK_DEV).astype(jnp.bfloat16)
    token_grad = lax.map(block_grad, (per_block, slot_token.astype(jnp.int32))).reshape(TOKENS, D)
    gate_grad = jnp.transpose(gate_sums, (1, 0, 2)).reshape(D, FLIGHT * FF).astype(jnp.bfloat16)
    up_grad = jnp.transpose(up_sums, (1, 0, 2)).reshape(D, FLIGHT * FF).astype(jnp.bfloat16)
    down_grad = down_sums.reshape(FLIGHT * FF, D).astype(jnp.bfloat16)
    return (token_grad, gate_grad, up_grad, down_grad)
```

```python
import jax
import jax.numpy as jnp
from jax import lax
from jax.experimental import pallas as pl
from jax.experimental.pallas import tpu as pltpu
from jax.sharding import PartitionSpec as P

F32 = jnp.float32
BF16 = jnp.bfloat16
MESH = pl.DeviceIdType.MESH

X = 4
Y = 8
Z = 16
D = 4096
HALF = D // 2
FLIGHT = 8
TOK = 128
HD = 128
BLOCK = 16
ROWS = BLOCK * X
SLICE = 256
GRADS = 3 * HD
PIECES = 4
PIECE = GRADS // PIECES
MID = HALF // 2


def lanes(a, b):
    return lax.dot_general(a, b, (((1,), (1,)), ((), ())), preferred_element_type=F32)


def dot(a, b):
    return jnp.dot(a, b, preferred_element_type=F32)


def kernel(
    st, sg, tok_hbm, cot_hbm, wg_hbm, wu_hbm, wd_hbm,
    tg_out, gg_out, ug_out, dg_out,
    tok, cot, w, wd, tile, tile2, merged, give, got, zin, rows, dab, gt,
    part, d2d, rout, rin, pz_out, pz_in, pm, pa_out, pa_in, pb_out, pb_in,
    zq_out, zq_in, pq_in, prow,
    load_sem, pair_s, pair_r, z_s, z_r, ag_s, ag_r, d2d_s, d2d_r, ring_s, ring_r,
    pz_sem, pa_s, pa_r, pb_s, pb_r, zq_sem, pq_sem,
):
    d = lax.axis_index("dp")
    e = lax.axis_index("expert")
    y, core = d // 2, d % 2
    z, x = e // X, e % X
    h = z % 2
    other_core = {"dp": y * 2 + 1 - core}
    y_next = {"dp": (y + 1) % Y * 2 + core}
    y_prev = {"dp": (y + Y - 1) % Y * 2 + core}
    x_next = {"expert": z * X + (x + 1) % X}
    x_prev = {"expert": z * X + (x + X - 1) % X}
    x_pair = {"expert": e + 1 - 2 * (x % 2)}
    z_pair = {"expert": e + X - 2 * X * h}

    def remote(src, dst, send_sem, recv_sem, to):
        return pltpu.make_async_remote_copy(
            src_ref=src, dst_ref=dst, send_sem=send_sem, recv_sem=recv_sem,
            device_id=to, device_id_type=MESH,
        )

    sent = []

    def send(src, dst, send_sem, recv_sem, to):
        copy = remote(src, dst, send_sem, recv_sem, to)
        copy.start()
        sent.append(copy)

    def arrived(dst, recv_sem):
        remote(dst, dst, recv_sem, recv_sem, other_core).wait_recv()

    barrier = pltpu.get_barrier_semaphore()

    def z_at(i):
        return (z + i) % Z

    def greet(i, carry):
        pl.semaphore_signal(
            barrier, inc=1, device_id={"expert": z_at(i) * X + x}, device_id_type=MESH
        )
        return carry

    for to in (x_next, x_prev, other_core, y_next, y_prev):
        pl.semaphore_signal(barrier, inc=1, device_id=to, device_id_type=MESH)
    lax.fori_loop(1, Z, greet, 0)

    loads = [
        pltpu.make_async_copy(src, dst, load_sem.at[i])
        for i, (src, dst) in enumerate(
            (
                (tok_hbm, tok),
                (cot_hbm, cot),
                (wg_hbm, w.at[:, 0:HD]),
                (wu_hbm, w.at[:, HD : 2 * HD]),
                (wd_hbm, wd),
            )
        )
    ]
    for copy in loads:
        copy.start()

    line = lax.broadcasted_iota(jnp.int32, (BLOCK, TOK), 0)
    lane = lax.broadcasted_iota(jnp.int32, (BLOCK, TOK), 1)
    row_t = lax.broadcasted_iota(jnp.int32, (TOK, BLOCK), 0)
    col_t = lax.broadcasted_iota(jnp.int32, (TOK, BLOCK), 1)
    pick = jnp.zeros((BLOCK, TOK), F32)
    pick_t = jnp.zeros((TOK, BLOCK), F32)
    weight = jnp.zeros((BLOCK, TOK), F32)
    for k in range(2):
        for f in range(FLIGHT):
            s = k * FLIGHT + f
            code = sg[0, f * 2 + k]
            token = jnp.where(code != 0, st[0, f * 2 + k], -1)
            pick = jnp.where((line == s) & (lane == token), 1.0, pick)
            pick_t = jnp.where((col_t == s) & (row_t == token), 1.0, pick_t)
            weight = jnp.where(line == s, code.astype(F32) / 1024.0, weight)
    pick = pick.astype(BF16)
    pick_t = pick_t.astype(BF16)

    def select(stage):
        source = (tok, cot)[stage]
        loads[stage].wait()
        chosen = dot(pick, source[...])
        if stage == 1:
            chosen = chosen * weight[:, 0:1]
        for c in range(D // 128):
            tile[c * BLOCK : (c + 1) * BLOCK, :] = chosen[:, c * 128 : (c + 1) * 128]
        for s in range(BLOCK):
            target = merged if s < FLIGHT else give
            f = s % FLIGHT
            value = tile[pl.ds(s, D // 128, stride=BLOCK), :].astype(BF16)
            target[stage, 2 * f] = value[0:16]
            target[stage, 2 * f + 1] = value[16:32]

    def give_pair(stage):
        send(give.at[stage], got.at[stage], pair_s.at[stage], pair_r.at[stage], x_pair)

    def all_z(stage, src, dst, send_sem, recv_sem):
        def body(i, carry):
            step = jnp.where(i % 2 == 1, (i + 1) // 2, Z - i // 2)
            zt = z_at(step)
            remote(src.at[zt], dst.at[z], send_sem, recv_sem, {"expert": zt * X + x}).start()
            return carry

        lax.fori_loop(1, Z, body, 0)
        dst[z] = src[z]
        sent.append(remote(src.at[pl.ds(0, Z - 1)], src.at[pl.ds(0, Z - 1)], send_sem, recv_sem, x_next))

    def merge(stage):
        arrived(got.at[stage], pair_r.at[stage])
        merged[stage] = merged[stage] + got[stage]
        all_z(stage, merged.at[stage], zin.at[stage], z_s.at[stage], z_r.at[stage])

    def place(stage, half, column):
        start = pl.multiple_of((column + X) % X * BLOCK, BLOCK)
        return rows.at[stage, half, pl.ds(start, BLOCK), :]

    def gather(stage):
        arrived(zin.at[stage, pl.ds(0, Z - 1)], z_r.at[stage])
        for i in range(Z):
            tile2[pl.ds(i, 16, stride=Z), :] = zin[stage, i].astype(F32)
        mine = place(stage, h, x)
        for c in range(HALF // 128):
            mine[:, c * 128 : (c + 1) * 128] = tile2[c * BLOCK : (c + 1) * BLOCK, :].astype(BF16)

        def hand(ref, i, to):
            send(ref, ref, ag_s.at[stage, i], ag_r.at[stage, i], to)

        hand(mine, 0, z_pair)
        hand(mine, 1, x_next)
        hand(mine, 2, x_prev)

    def gather_on(stage):
        def hand(ref, i, to):
            send(ref, ref, ag_s.at[stage, i], ag_r.at[stage, i], to)

        def take(ref, i):
            arrived(ref, ag_r.at[stage, i])

        twin = place(stage, 1 - h, x)
        take(twin, 0)
        hand(twin, 3, x_next)
        hand(twin, 4, x_prev)
        left = place(stage, h, x - 1)
        take(left, 1)
        hand(left, 5, x_next)
        right = place(stage, 1 - h, x + 1)
        take(right, 4)
        hand(right, 6, x_prev)
        take(place(stage, h, x + 1), 2)
        take(place(stage, 1 - h, x - 1), 3)
        take(place(stage, h, x + 2), 5)
        take(place(stage, 1 - h, x + 2), 6)

    select(0)
    pl.semaphore_wait(barrier, Z + 4)
    give_pair(0)
    select(1)
    give_pair(1)
    merge(0)
    merge(1)
    gather(0)
    gather(1)
    gather_on(0)
    for copy in loads[2:]:
        copy.wait()
    ab = dot(rows[0, 0], w[0:HALF, :]) + dot(rows[0, 1], w[HALF:D, :])
    gather_on(1)
    dh = lanes(rows[1, 0], wd[:, 0:HALF]) + lanes(rows[1, 1], wd[:, HALF:D])
    a, b = ab[:, 0:HD], ab[:, HD : 2 * HD]
    sig = 1.0 / (1.0 + jnp.exp(-a))
    act = a * sig
    grads = jnp.concatenate(
        (dh * b * sig * (1.0 + a * (1.0 - sig)), dh * act, act * b), axis=1
    )
    dab[...] = grads[:, 0 : 2 * HD].astype(BF16)
    gt[...] = jnp.transpose(grads).astype(BF16)

    def partial(far):
        yt = (y + far) % Y
        half = yt // 4
        cols = pl.ds(pl.multiple_of(yt % 4 * (2 * SLICE), 2 * SLICE), 2 * SLICE)
        gu = dot(gt[0 : 2 * HD, :], rows[0, half, :, cols])
        dn = dot(gt[2 * HD : GRADS, :], rows[1, half, :, cols])
        for c in range(2):
            part[far, c, 0 : 2 * HD, :] = gu[:, c * SLICE : (c + 1) * SLICE].astype(BF16)
            part[far, c, 2 * HD : GRADS, :] = dn[:, c * SLICE : (c + 1) * SLICE].astype(BF16)
        send(part.at[far, 1 - core], d2d.at[far], d2d_s.at[far], d2d_r.at[far], other_core)

    def both_cores(far):
        arrived(d2d.at[far], d2d_r.at[far])

    def own(far, piece):
        lo = piece * PIECE
        return part[far, core, lo : lo + PIECE, :].astype(F32) + d2d[far, lo : lo + PIECE, :].astype(F32)

    def ring(way, hops, piece):
        far = hops if way == 0 else Y - hops
        value = own(far, piece)
        if hops < 3 or (hops == 3 and piece // 2 == way):
            arrived(rin.at[way, hops, piece], ring_r.at[way, hops, piece])
            value = value + rin[way, hops, piece].astype(F32)
        rout[way, hops - 1, piece] = value.astype(BF16)
        send(
            rout.at[way, hops - 1, piece], rin.at[way, hops - 1, piece],
            ring_s.at[way, hops - 1, piece], ring_r.at[way, hops - 1, piece],
            y_next if way == 0 else y_prev,
        )

    def ring_step(hops, late):
        for i in range(2):
            for way in range(2):
                side = way if late else 1 - way
                ring(way, hops, 2 * side + i)

    def p_far():
        lo = pl.multiple_of((1 - h) * HALF, HALF)
        pz_out[...] = lanes(dab[...], w[pl.ds(lo, HALF), :]).astype(BF16)
        send(pz_out, pz_in, pz_sem.at[0], pz_sem.at[1], z_pair)

    def p_near():
        lo = pl.multiple_of(h * HALF, HALF)
        pm[...] = lanes(dab[...], w[pl.ds(lo, HALF), :])

    def p_rows(column, c):
        start = pl.multiple_of((column + X) % X * BLOCK, BLOCK)
        return pm[pl.ds(start, BLOCK), c * MID : (c + 1) * MID]

    def p_a():
        arrived(pz_in, pz_sem.at[1])
        pm[...] = pm[...] + pz_in[...].astype(F32)
        for way in range(2):
            pa_out[way] = p_rows(x + 2, way).astype(BF16)
            send(pa_out.at[way], pa_in.at[way], pa_s.at[way], pa_r.at[way], (x_next, x_prev)[way])
        for way in range(2):
            p_b(way, 1 - way)

    def p_b(way, c):
        value = p_rows(x + 1 if way == 0 else x - 1, c)
        if c == way:
            arrived(pa_in.at[way], pa_r.at[way])
            value = value + pa_in[way].astype(F32)
        pb_out[way, c] = value.astype(BF16)
        send(
            pb_out.at[way, c], pb_in.at[way, c], pb_s.at[way, c], pb_r.at[way, c],
            (x_next, x_prev)[way],
        )

    def p_back():
        for c in range(2):
            value = p_rows(x, c)
            for way in (1 - c, c):
                arrived(pb_in.at[way, c], pb_r.at[way, c])
                value = value + pb_in[way, c].astype(F32)
            for i in range(MID // 128):
                lo = (c * (MID // 128) + i) * BLOCK
                tile2[lo : lo + BLOCK, :] = value[:, i * 128 : (i + 1) * 128]
        for i in range(Z):
            zq_out[i] = tile2[pl.ds(i, 16, stride=Z), :].astype(BF16)
        all_z(0, zq_out, zq_in, zq_sem.at[0], zq_sem.at[1])

    def p_pair():
        arrived(zq_in.at[pl.ds(0, Z - 1)], zq_sem.at[1])
        send(zq_in, pq_in, pq_sem.at[0], pq_sem.at[1], x_pair)

    def p_tokens():
        for f in range(FLIGHT):
            for half in range(2):
                tile[pl.ds(half * 256 + f, 16, stride=BLOCK), :] = zq_in[2 * f + half].astype(F32)
        arrived(pq_in, pq_sem.at[1])
        for f in range(FLIGHT):
            for half in range(2):
                tile[pl.ds(half * 256 + FLIGHT + f, 16, stride=BLOCK), :] = pq_in[2 * f + half].astype(F32)
        for c in range(D // 128):
            prow[:, c * 128 : (c + 1) * 128] = tile[c * BLOCK : (c + 1) * BLOCK, :].astype(BF16)
        tg_out[...] = dot(pick_t, prow[...]).astype(BF16)

    partial(4)
    partial(3)
    partial(5)
    p_far()
    both_cores(4)
    for i in range(2):
        ring(0, 4, i)
        ring(1, 4, 2 + i)
    both_cores(3)
    both_cores(5)
    ring_step(3, False)
    partial(2)
    partial(6)
    ring_step(3, True)
    partial(1)
    partial(7)
    partial(0)
    p_near()
    both_cores(2)
    both_cores(6)
    ring_step(2, False)
    p_a()
    ring_step(2, True)
    for way in range(2):
        p_b(way, way)
    both_cores(1)
    both_cores(7)
    ring_step(1, False)
    p_back()
    ring_step(1, True)
    both_cores(0)
    p_pair()
    p_tokens()

    totals = []
    for piece in range(PIECES):
        value = own(0, piece)
        for way in range(2):
            arrived(rin.at[way, 0, piece], ring_r.at[way, 0, piece])
            value = value + rin[way, 0, piece].astype(F32)
        totals.append(value)
    total = jnp.concatenate(totals, axis=0)
    gg_out[...] = jnp.transpose(total[0:HD]).astype(BF16)
    ug_out[...] = jnp.transpose(total[HD : 2 * HD]).astype(BF16)
    dg_out[...] = total[2 * HD : GRADS].astype(BF16)
    for copy in sent:
        copy.wait_send()


def shards(tokens, cotangent, slot_token, slot_gate, gate_weight, up_weight, down_weight):
    any_space = pl.BlockSpec(memory_space=pl.ANY)
    vmem = pl.BlockSpec(memory_space=pltpu.VMEM)
    smem = pl.BlockSpec(memory_space=pltpu.SMEM)
    dma = pltpu.SemaphoreType.DMA
    return pl.pallas_call(
        kernel,
        out_shape=(
            jax.ShapeDtypeStruct((TOK, D), BF16),
            jax.ShapeDtypeStruct((SLICE, HD), BF16),
            jax.ShapeDtypeStruct((SLICE, HD), BF16),
            jax.ShapeDtypeStruct((HD, SLICE), BF16),
        ),
        in_specs=[smem, smem] + [any_space] * 5,
        out_specs=(vmem,) * 4,
        scratch_shapes=[
            pltpu.VMEM((TOK, D), BF16),
            pltpu.VMEM((TOK, D), BF16),
            pltpu.VMEM((D, 2 * HD), BF16),
            pltpu.VMEM((HD, D), BF16),
            pltpu.VMEM((D // 128 * BLOCK, 128), F32),
            pltpu.VMEM((HALF // 128 * BLOCK, 128), F32),
            pltpu.VMEM((2, Z, 16, 128), BF16),
            pltpu.VMEM((2, Z, 16, 128), BF16),
            pltpu.VMEM((2, Z, 16, 128), BF16),
            pltpu.VMEM((2, Z, 16, 128), BF16),
            pltpu.VMEM((2, 2, ROWS, HALF), BF16),
            pltpu.VMEM((ROWS, 2 * HD), BF16),
            pltpu.VMEM((GRADS, ROWS), BF16),
            pltpu.VMEM((Y, 2, GRADS, SLICE), BF16),
            pltpu.VMEM((Y, GRADS, SLICE), BF16),
            pltpu.VMEM((2, 4, PIECES, PIECE, SLICE), BF16),
            pltpu.VMEM((2, 4, PIECES, PIECE, SLICE), BF16),
            pltpu.VMEM((ROWS, HALF), BF16),
            pltpu.VMEM((ROWS, HALF), BF16),
            pltpu.VMEM((ROWS, HALF), F32),
            pltpu.VMEM((2, BLOCK, MID), BF16),
            pltpu.VMEM((2, BLOCK, MID), BF16),
            pltpu.VMEM((2, 2, BLOCK, MID), BF16),
            pltpu.VMEM((2, 2, BLOCK, MID), BF16),
            pltpu.VMEM((Z, 16, 128), BF16),
            pltpu.VMEM((Z, 16, 128), BF16),
            pltpu.VMEM((Z, 16, 128), BF16),
            pltpu.VMEM((BLOCK, D), BF16),
            dma((5,)),
            dma((2,)),
            dma((2,)),
            dma((2,)),
            dma((2,)),
            dma((2, 7)),
            dma((2, 7)),
            dma((Y,)),
            dma((Y,)),
            dma((2, 4, PIECES)),
            dma((2, 4, PIECES)),
            dma((2,)),
            dma((2,)),
            dma((2,)),
            dma((2, 2)),
            dma((2, 2)),
            dma((2,)),
            dma((2,)),
        ],
        compiler_params=pltpu.CompilerParams(
            collective_id=0, has_side_effects=True, vmem_limit_bytes=40 * 1024 * 1024
        ),
        name="moe_backward",
    )(slot_token, slot_gate, tokens, cotangent, gate_weight, up_weight, down_weight)


def solution(mesh):
    placed = (
        P(("dp", "expert"), None),
        P(("dp", "expert"), None),
        P(("dp", "expert"), None),
        P(("dp", "expert"), None),
        P(None, "expert"),
        P(None, "expert"),
        P("expert", None),
    )
    return jax.shard_map(
        shards,
        mesh=mesh,
        in_specs=placed,
        out_specs=(
            P(("dp", "expert"), None),
            P("dp", "expert"),
            P("dp", "expert"),
            P("expert", "dp"),
        ),
        check_vma=False,
    )
```

```python
import jax
import jax.numpy as jnp
from jax import lax
from jax.experimental import pallas as pl
from jax.experimental.pallas import tpu as pltpu
from jax.sharding import PartitionSpec as P

F32 = jnp.float32
BF16 = jnp.bfloat16
MESH = pl.DeviceIdType.MESH

X = 4
Y = 8
Z = 16
D = 4096
HALF = D // 2
FLIGHT = 8
TOK = 128
HD = 128
BLOCK = 16
ROWS = BLOCK * X
SLICE = 256
GRADS = 3 * HD
PIECES = 4
PIECE = GRADS // PIECES
MID = HALF // 2


def lanes(a, b):
    return lax.dot_general(a, b, (((1,), (1,)), ((), ())), preferred_element_type=F32)


def dot(a, b):
    return jnp.dot(a, b, preferred_element_type=F32)


def kernel(
    st_hbm, sg_hbm, tok_hbm, cot_hbm, wg_hbm, wu_hbm, wd_hbm,
    prow, pick_out, total_out,
    st, sg, tok, cot, w, wd, tile, tile2, merged, give, got, zin, rows, dab, gt,
    part, d2d, rout, rin, pz_out, pz_in, pm, pa_out, pa_in, pb_out, pb_in,
    zq_out, zq_in, pq_in,
    load_sem, pair_s, pair_r, z_s, z_r, ag_s, ag_r, d2d_s, d2d_r, ring_s, ring_r,
    pz_s, pz_r, pa_s, pa_r, pb_s, pb_r, zq_sem, pq_sem,
):
    d = lax.axis_index("dp")
    e = lax.axis_index("expert")
    y, core = d // 2, d % 2
    z, x = e // X, e % X
    h = z % 2
    other_core = {"dp": y * 2 + 1 - core}
    y_next = {"dp": (y + 1) % Y * 2 + core}
    y_prev = {"dp": (y + Y - 1) % Y * 2 + core}
    x_next = {"expert": z * X + (x + 1) % X}
    x_prev = {"expert": z * X + (x + X - 1) % X}
    x_pair = {"expert": e + 1 - 2 * (x % 2)}
    z_pair = {"expert": e + X - 2 * X * h}

    def remote(src, dst, send_sem, recv_sem, to):
        return pltpu.make_async_remote_copy(
            src_ref=src, dst_ref=dst, send_sem=send_sem, recv_sem=recv_sem,
            device_id=to, device_id_type=MESH,
        )

    sent = []

    def send(src, dst, send_sem, recv_sem, to):
        copy = remote(src, dst, send_sem, recv_sem, to)
        copy.start()
        sent.append(copy)

    def arrived(dst, recv_sem):
        remote(dst, dst, recv_sem, recv_sem, other_core).wait_recv()

    barrier = pltpu.get_barrier_semaphore()

    def z_at(i):
        return (z + i) % Z

    def greet(i, carry):
        pl.semaphore_signal(
            barrier, inc=1, device_id={"expert": z_at(i) * X + x}, device_id_type=MESH
        )
        return carry

    for to in (x_next, x_prev, other_core, y_next, y_prev):
        pl.semaphore_signal(barrier, inc=1, device_id=to, device_id_type=MESH)
    lax.fori_loop(1, Z, greet, 0)

    loads = [
        pltpu.make_async_copy(src, dst, load_sem.at[i])
        for i, (src, dst) in enumerate(
            (
                (st_hbm, st),
                (sg_hbm, sg),
                (tok_hbm, tok),
                (cot_hbm, cot),
                (wg_hbm, w.at[:, 0:HD]),
                (wu_hbm, w.at[:, HD : 2 * HD]),
                (wd_hbm, wd),
            )
        )
    ]
    for copy in loads:
        copy.start()

    loads[0].wait()
    loads[1].wait()

    line = lax.broadcasted_iota(jnp.int32, (BLOCK, TOK), 0)
    lane = lax.broadcasted_iota(jnp.int32, (BLOCK, TOK), 1)
    row_t = lax.broadcasted_iota(jnp.int32, (TOK, BLOCK), 0)
    col_t = lax.broadcasted_iota(jnp.int32, (TOK, BLOCK), 1)
    pick = jnp.zeros((BLOCK, TOK), F32)
    pick_t = jnp.zeros((TOK, BLOCK), F32)
    weight = jnp.zeros((BLOCK, TOK), F32)
    for k in range(2):
        for f in range(FLIGHT):
            s = k * FLIGHT + f
            code = sg[0, f * 2 + k]
            token = jnp.where(code != 0, st[0, f * 2 + k], -1)
            pick = jnp.where((line == s) & (lane == token), 1.0, pick)
            pick_t = jnp.where((col_t == s) & (row_t == token), 1.0, pick_t)
            weight = jnp.where(line == s, code.astype(F32) / 1024.0, weight)
    pick = pick.astype(BF16)
    pick_out[...] = pick_t.astype(BF16)

    def select(stage):
        source = (tok, cot)[stage]
        loads[2 + stage].wait()
        chosen = dot(pick, source[...])
        if stage == 1:
            chosen = chosen * weight[:, 0:1]
        for c in range(D // 128):
            tile[c * BLOCK : (c + 1) * BLOCK, :] = chosen[:, c * 128 : (c + 1) * 128]
        for s in range(BLOCK):
            target = merged if s < FLIGHT else give
            f = s % FLIGHT
            value = tile[pl.ds(s, D // 128, stride=BLOCK), :].astype(BF16)
            target[stage, 2 * f] = value[0:16]
            target[stage, 2 * f + 1] = value[16:32]

    def give_pair(stage):
        send(give.at[stage], got.at[stage], pair_s.at[stage], pair_r.at[stage], x_pair)

    def all_z(stage, src, dst, send_sem, recv_sem):
        def body(i, carry):
            step = jnp.where(i % 2 == 1, (i + 1) // 2, Z - i // 2)
            zt = z_at(step)
            remote(src.at[zt], dst.at[z], send_sem, recv_sem, {"expert": zt * X + x}).start()
            return carry

        lax.fori_loop(1, Z, body, 0)
        dst[z] = src[z]
        sent.append(remote(src.at[pl.ds(0, Z - 1)], src.at[pl.ds(0, Z - 1)], send_sem, recv_sem, x_next))

    def merge(stage):
        arrived(got.at[stage], pair_r.at[stage])
        merged[stage] = merged[stage] + got[stage]
        all_z(stage, merged.at[stage], zin.at[stage], z_s.at[stage], z_r.at[stage])

    def place(stage, half, column, lo=0, width=HALF):
        start = pl.multiple_of((column + X) % X * BLOCK, BLOCK)
        return rows.at[stage, half, pl.ds(start, BLOCK), pl.ds(lo, width)]

    def hand(stage, ref, i, to):
        send(ref, ref, ag_s.at[stage, i], ag_r.at[stage, i], to)

    def take(stage, ref, i):
        arrived(ref, ag_r.at[stage, i])

    def gather(stage):
        arrived(zin.at[stage, pl.ds(0, Z - 1)], z_r.at[stage])
        for i in range(Z):
            tile2[pl.ds(i, 16, stride=Z), :] = zin[stage, i].astype(F32)
        mine = place(stage, h, x)
        for c in range(HALF // 128):
            mine[:, c * 128 : (c + 1) * 128] = tile2[c * BLOCK : (c + 1) * BLOCK, :].astype(BF16)
        hand(stage, mine, 0, z_pair)
        hand(stage, mine, 1, x_next)
        hand(stage, mine, 2, x_prev)

    def gather_far(stage):
        take(stage, place(stage, h, x - 1), 1)
        hand(stage, place(stage, h, x - 1, 0, MID), 5, x_next)
        take(stage, place(stage, h, x + 1), 2)
        hand(stage, place(stage, h, x + 1, MID, MID), 6, x_prev)

    def gather_twin(stage):
        twin = place(stage, 1 - h, x)
        take(stage, twin, 0)
        hand(stage, twin, 3, x_next)
        hand(stage, twin, 4, x_prev)

    def gather_cross(stage):
        for i in range(2):
            far = place(stage, h, x + 2, i * MID, MID)
            take(stage, far, 5 + i)
            hand(stage, far, 7 + i, z_pair)

    def gather_end(stage):
        take(stage, place(stage, 1 - h, x - 1), 3)
        take(stage, place(stage, 1 - h, x + 1), 4)
        for i in range(2):
            take(stage, place(stage, 1 - h, x + 2, i * MID, MID), 7 + i)

    select(0)
    pl.semaphore_wait(barrier, Z + 4)
    give_pair(0)
    select(1)
    give_pair(1)
    merge(0)
    merge(1)
    gather(0)
    gather(1)
    gather_far(0)
    gather_far(1)
    gather_twin(0)
    gather_twin(1)
    gather_cross(0)
    gather_cross(1)
    gather_end(0)
    for copy in loads[4:]:
        copy.wait()
    ab = dot(rows[0, 0], w[0:HALF, :]) + dot(rows[0, 1], w[HALF:D, :])
    gather_end(1)
    dh = lanes(rows[1, 0], wd[:, 0:HALF]) + lanes(rows[1, 1], wd[:, HALF:D])
    a, b = ab[:, 0:HD], ab[:, HD : 2 * HD]
    sig = 1.0 / (1.0 + jnp.exp(-a))
    act = a * sig
    grads = jnp.concatenate(
        (dh * b * sig * (1.0 + a * (1.0 - sig)), dh * act, act * b), axis=1
    )
    dab[...] = grads[:, 0 : 2 * HD].astype(BF16)
    gt[...] = jnp.transpose(grads).astype(BF16)

    def partial(far):
        yt = (y + far) % Y
        half = yt // 4
        cols = pl.ds(pl.multiple_of(yt % 4 * (2 * SLICE), 2 * SLICE), 2 * SLICE)
        gu = dot(gt[0 : 2 * HD, :], rows[0, half, :, cols])
        dn = dot(gt[2 * HD : GRADS, :], rows[1, half, :, cols])
        for c in range(2):
            part[far, c, 0 : 2 * HD, :] = gu[:, c * SLICE : (c + 1) * SLICE].astype(BF16)
            part[far, c, 2 * HD : GRADS, :] = dn[:, c * SLICE : (c + 1) * SLICE].astype(BF16)
        send(part.at[far, 1 - core], d2d.at[far], d2d_s.at[far], d2d_r.at[far], other_core)

    def both_cores(far):
        arrived(d2d.at[far], d2d_r.at[far])

    def own(far, piece):
        lo = piece * PIECE
        return part[far, core, lo : lo + PIECE, :].astype(F32) + d2d[far, lo : lo + PIECE, :].astype(F32)

    def ring(way, hops, piece):
        far = hops if way == 0 else Y - hops
        value = own(far, piece)
        if hops < 3 or (hops == 3 and piece // 2 == way):
            arrived(rin.at[way, hops, piece], ring_r.at[way, hops, piece])
            value = value + rin[way, hops, piece].astype(F32)
        rout[way, hops - 1, piece] = value.astype(BF16)
        send(
            rout.at[way, hops - 1, piece], rin.at[way, hops - 1, piece],
            ring_s.at[way, hops - 1, piece], ring_r.at[way, hops - 1, piece],
            y_next if way == 0 else y_prev,
        )

    def ring_step(hops, late):
        for i in range(2):
            for way in range(2):
                side = way if late else 1 - way
                ring(way, hops, 2 * side + i)

    def p_place(ref, column):
        start = pl.multiple_of((column + X) % X * BLOCK, BLOCK)
        return ref.at[pl.ds(start, BLOCK), :]

    p_order = (x + 2, x + 1, x - 1, x)

    def p_far():
        lo = pl.multiple_of((1 - h) * HALF, HALF)
        pz_out[...] = lanes(dab[...], w[pl.ds(lo, HALF), :]).astype(BF16)
        for i, column in enumerate(p_order):
            send(
                p_place(pz_out, column), p_place(pz_in, column), pz_s.at[i], pz_r.at[i], z_pair
            )

    def p_near():
        lo = pl.multiple_of(h * HALF, HALF)
        pm[...] = lanes(dab[...], w[pl.ds(lo, HALF), :])

    def p_sum(i):
        arrived(p_place(pz_in, p_order[i]), pz_r.at[i])
        return p_place(pm, p_order[i])[...] + p_place(pz_in, p_order[i])[...].astype(F32)

    def p_a():
        value = p_sum(0)
        for way in range(2):
            pa_out[way] = value[:, way * MID : (way + 1) * MID].astype(BF16)
            send(pa_out.at[way], pa_in.at[way], pa_s.at[way], pa_r.at[way], (x_next, x_prev)[way])

    def p_b():
        for way in range(2):
            value = p_sum(1 + way)
            for c in (1 - way, way):
                piece = value[:, c * MID : (c + 1) * MID]
                if c == way:
                    arrived(pa_in.at[way], pa_r.at[way])
                    piece = piece + pa_in[way].astype(F32)
                pb_out[way, c] = piece.astype(BF16)
                send(
                    pb_out.at[way, c], pb_in.at[way, c], pb_s.at[way, c], pb_r.at[way, c],
                    (x_next, x_prev)[way],
                )

    def p_back():
        mine = p_sum(3)
        for c in range(2):
            value = mine[:, c * MID : (c + 1) * MID]
            for way in (1 - c, c):
                arrived(pb_in.at[way, c], pb_r.at[way, c])
                value = value + pb_in[way, c].astype(F32)
            for i in range(MID // 128):
                lo = (c * (MID // 128) + i) * BLOCK
                tile2[lo : lo + BLOCK, :] = value[:, i * 128 : (i + 1) * 128]
        for i in range(Z):
            zq_out[i] = tile2[pl.ds(i, 16, stride=Z), :].astype(BF16)
        all_z(0, zq_out, zq_in, zq_sem.at[0], zq_sem.at[1])

    def p_pair():
        arrived(zq_in.at[pl.ds(0, Z - 1)], zq_sem.at[1])
        send(zq_in, pq_in, pq_sem.at[0], pq_sem.at[1], x_pair)

    def p_tokens():
        for f in range(FLIGHT):
            for half in range(2):
                tile[pl.ds(half * 256 + f, 16, stride=BLOCK), :] = zq_in[2 * f + half].astype(F32)
        arrived(pq_in, pq_sem.at[1])
        for f in range(FLIGHT):
            for half in range(2):
                tile[pl.ds(half * 256 + FLIGHT + f, 16, stride=BLOCK), :] = pq_in[2 * f + half].astype(F32)
        for c in range(D // 128):
            prow[:, c * 128 : (c + 1) * 128] = tile[c * BLOCK : (c + 1) * BLOCK, :].astype(BF16)

    partial(4)
    p_far()
    partial(3)
    partial(5)
    both_cores(4)
    for i in range(2):
        ring(0, 4, i)
        ring(1, 4, 2 + i)
    both_cores(3)
    both_cores(5)
    ring_step(3, False)
    p_near()
    partial(2)
    partial(6)
    p_a()
    partial(1)
    partial(7)
    partial(0)
    ring_step(3, True)
    p_b()
    both_cores(2)
    both_cores(6)
    ring_step(2, False)
    p_back()
    ring_step(2, True)
    both_cores(1)
    both_cores(7)
    ring_step(1, False)
    ring_step(1, True)
    p_pair()
    both_cores(0)
    for piece in range(PIECES):
        value = own(0, piece)
        for way in range(2):
            arrived(rin.at[way, 0, piece], ring_r.at[way, 0, piece])
            value = value + rin[way, 0, piece].astype(F32)
        total_out[piece * PIECE : (piece + 1) * PIECE, :] = value
    p_tokens()
    for copy in sent:
        copy.wait_send()


def finish(prow, pick_t, total, tg_hbm, gg_hbm, ug_hbm, dg_hbm, tg, gg, ug, dg, sems):
    copies = []

    def out(src, dst):
        copies.append(pltpu.make_async_copy(src, dst, sems.at[len(copies)]))
        copies[-1].start()

    for c in range(4):
        cols = slice(c * (D // 4), (c + 1) * (D // 4))
        tg[:, cols] = dot(pick_t[...], prow[:, cols]).astype(BF16)
        out(tg.at[:, cols], tg_hbm.at[:, cols])
    dg[...] = total[2 * HD : GRADS, :].astype(BF16)
    out(dg, dg_hbm)
    gg[...] = jnp.transpose(total[0:HD, :]).astype(BF16)
    out(gg, gg_hbm)
    ug[...] = jnp.transpose(total[HD : 2 * HD, :]).astype(BF16)
    out(ug, ug_hbm)
    for copy in copies:
        copy.wait()


def shards(tokens, cotangent, slot_token, slot_gate, gate_weight, up_weight, down_weight):
    hbm = pl.BlockSpec(memory_space=pltpu.HBM)
    vmem = pl.BlockSpec(memory_space=pltpu.VMEM)
    dma = pltpu.SemaphoreType.DMA
    prow, pick_t, total = pl.pallas_call(
        kernel,
        out_shape=(
            jax.ShapeDtypeStruct((BLOCK, D), BF16),
            jax.ShapeDtypeStruct((TOK, BLOCK), BF16),
            jax.ShapeDtypeStruct((GRADS, SLICE), F32),
        ),
        in_specs=[hbm] * 7,
        out_specs=(vmem,) * 3,
        scratch_shapes=[
            pltpu.SMEM((1, 2 * FLIGHT), jnp.int32),
            pltpu.SMEM((1, 2 * FLIGHT), jnp.int32),
            pltpu.VMEM((TOK, D), BF16),
            pltpu.VMEM((TOK, D), BF16),
            pltpu.VMEM((D, 2 * HD), BF16),
            pltpu.VMEM((HD, D), BF16),
            pltpu.VMEM((D // 128 * BLOCK, 128), F32),
            pltpu.VMEM((HALF // 128 * BLOCK, 128), F32),
            pltpu.VMEM((2, Z, 16, 128), BF16),
            pltpu.VMEM((2, Z, 16, 128), BF16),
            pltpu.VMEM((2, Z, 16, 128), BF16),
            pltpu.VMEM((2, Z, 16, 128), BF16),
            pltpu.VMEM((2, 2, ROWS, HALF), BF16),
            pltpu.VMEM((ROWS, 2 * HD), BF16),
            pltpu.VMEM((GRADS, ROWS), BF16),
            pltpu.VMEM((Y, 2, GRADS, SLICE), BF16),
            pltpu.VMEM((Y, GRADS, SLICE), BF16),
            pltpu.VMEM((2, 4, PIECES, PIECE, SLICE), BF16),
            pltpu.VMEM((2, 4, PIECES, PIECE, SLICE), BF16),
            pltpu.VMEM((ROWS, HALF), BF16),
            pltpu.VMEM((ROWS, HALF), BF16),
            pltpu.VMEM((ROWS, HALF), F32),
            pltpu.VMEM((2, BLOCK, MID), BF16),
            pltpu.VMEM((2, BLOCK, MID), BF16),
            pltpu.VMEM((2, 2, BLOCK, MID), BF16),
            pltpu.VMEM((2, 2, BLOCK, MID), BF16),
            pltpu.VMEM((Z, 16, 128), BF16),
            pltpu.VMEM((Z, 16, 128), BF16),
            pltpu.VMEM((Z, 16, 128), BF16),
            dma((7,)),
            dma((2,)),
            dma((2,)),
            dma((2,)),
            dma((2,)),
            dma((2, 9)),
            dma((2, 9)),
            dma((Y,)),
            dma((Y,)),
            dma((2, 4, PIECES)),
            dma((2, 4, PIECES)),
            dma((4,)),
            dma((4,)),
            dma((2,)),
            dma((2,)),
            dma((2, 2)),
            dma((2, 2)),
            dma((2,)),
            dma((2,)),
        ],
        compiler_params=pltpu.CompilerParams(
            collective_id=0, has_side_effects=True, vmem_limit_bytes=60 * 1024 * 1024
        ),
        name="moe_backward",
    )(slot_token, slot_gate, tokens, cotangent, gate_weight, up_weight, down_weight)

    shapes = ((TOK, D), (SLICE, HD), (SLICE, HD), (HD, SLICE))
    return pl.pallas_call(
        finish,
        out_shape=tuple(jax.ShapeDtypeStruct(shape, BF16) for shape in shapes),
        in_specs=[vmem] * 3,
        out_specs=(hbm,) * 4,
        scratch_shapes=[pltpu.VMEM(shape, BF16) for shape in shapes] + [dma((7,))],
        compiler_params=pltpu.CompilerParams(vmem_limit_bytes=60 * 1024 * 1024),
        name="finish",
    )(prow, pick_t, total)


def solution(mesh):
    placed = (
        P(("dp", "expert"), None),
        P(("dp", "expert"), None),
        P(("dp", "expert"), None),
        P(("dp", "expert"), None),
        P(None, "expert"),
        P(None, "expert"),
        P("expert", None),
    )
    return jax.shard_map(
        shards,
        mesh=mesh,
        in_specs=placed,
        out_specs=(
            P(("dp", "expert"), None),
            P("dp", "expert"),
            P("dp", "expert"),
            P("expert", "dp"),
        ),
        check_vma=False,
    )
```

```python
import jax
import jax.numpy as jnp
from jax import lax
from jax.experimental import pallas as pl
from jax.experimental.pallas import tpu as pltpu
from jax.sharding import PartitionSpec as P

F32 = jnp.float32
BF16 = jnp.bfloat16
MESH = pl.DeviceIdType.MESH

X = 4
Y = 8
Z = 16
D = 4096
HALF = D // 2
FLIGHT = 8
TOK = 128
HD = 128
BLOCK = 16
ROWS = BLOCK * X
SLICE = 256
GRADS = 3 * HD
PIECES = 4
PIECE = GRADS // PIECES
MID = HALF // 2


def lanes(a, b):
    return lax.dot_general(a, b, (((1,), (1,)), ((), ())), preferred_element_type=F32)


def dot(a, b):
    return jnp.dot(a, b, preferred_element_type=F32)


def kernel(
    st_hbm, sg_hbm, tok_hbm, cot_hbm, wg_hbm, wu_hbm, wd_hbm,
    prow, pick_out, total_out,
    st, sg, tok, cot, w, wd, tile, tile2, merged, give, got, zin, rows, dab, gt,
    part, d2d, rout, rin, pz_out, pz_in, pm, pa_out, pa_in, pb_out, pb_in,
    zq_out, zq_in, pq_in,
    load_sem, pair_s, pair_r, z_s, z_r, ag_s, ag_r, d2d_s, d2d_r, ring_s, ring_r,
    pz_s, pz_r, pa_s, pa_r, pb_s, pb_r, zq_sem, pq_sem, z_near,
):
    d = lax.axis_index("dp")
    e = lax.axis_index("expert")
    y, core = d // 2, d % 2
    z, x = e // X, e % X
    h = z % 2
    other_core = {"dp": y * 2 + 1 - core}
    y_next = {"dp": (y + 1) % Y * 2 + core}
    y_prev = {"dp": (y + Y - 1) % Y * 2 + core}
    x_next = {"expert": z * X + (x + 1) % X}
    x_prev = {"expert": z * X + (x + X - 1) % X}
    x_pair = {"expert": e + 1 - 2 * (x % 2)}
    z_pair = {"expert": e + X - 2 * X * h}

    def remote(src, dst, send_sem, recv_sem, to):
        return pltpu.make_async_remote_copy(
            src_ref=src, dst_ref=dst, send_sem=send_sem, recv_sem=recv_sem,
            device_id=to, device_id_type=MESH,
        )

    sent = []

    def send(src, dst, send_sem, recv_sem, to):
        copy = remote(src, dst, send_sem, recv_sem, to)
        copy.start()
        sent.append(copy)

    def arrived(dst, recv_sem):
        remote(dst, dst, recv_sem, recv_sem, other_core).wait_recv()

    barrier = pltpu.get_barrier_semaphore()

    def z_at(i):
        return (z + i) % Z

    def z_of(step):
        return {"expert": z_at(step + Z) * X + x}

    def greet(semaphore, to):
        pl.semaphore_signal(semaphore, inc=1, device_id=to, device_id_type=MESH)

    near = [z_of(way * step) for step in (4, 3, 2, 1) for way in (1, -1)]
    near += [x_next, x_prev, other_core, y_next, y_prev]
    for to in near:
        greet(barrier, to)

    loads = [
        pltpu.make_async_copy(src, dst, load_sem.at[i])
        for i, (src, dst) in enumerate(
            (
                (st_hbm, st),
                (sg_hbm, sg),
                (tok_hbm, tok),
                (cot_hbm, cot),
                (wg_hbm, w.at[:, 0:HD]),
                (wu_hbm, w.at[:, HD : 2 * HD]),
                (wd_hbm, wd),
            )
        )
    ]
    for copy in loads:
        copy.start()

    loads[0].wait()
    loads[1].wait()

    line = lax.broadcasted_iota(jnp.int32, (BLOCK, TOK), 0)
    lane = lax.broadcasted_iota(jnp.int32, (BLOCK, TOK), 1)
    row_t = lax.broadcasted_iota(jnp.int32, (TOK, BLOCK), 0)
    col_t = lax.broadcasted_iota(jnp.int32, (TOK, BLOCK), 1)
    pick = jnp.zeros((BLOCK, TOK), F32)
    pick_t = jnp.zeros((TOK, BLOCK), F32)
    weight = jnp.zeros((BLOCK, TOK), F32)
    for k in range(2):
        for f in range(FLIGHT):
            s = k * FLIGHT + f
            code = sg[0, f * 2 + k]
            token = jnp.where(code != 0, st[0, f * 2 + k], -1)
            pick = jnp.where((line == s) & (lane == token), 1.0, pick)
            pick_t = jnp.where((col_t == s) & (row_t == token), 1.0, pick_t)
            weight = jnp.where(line == s, code.astype(F32) / 1024.0, weight)
    pick = pick.astype(BF16)
    pick_out[...] = pick_t.astype(BF16)

    def select(stage):
        source = (tok, cot)[stage]
        loads[2 + stage].wait()
        chosen = dot(pick, source[...])
        if stage == 1:
            chosen = chosen * weight[:, 0:1]
        for c in range(D // 128):
            tile[c * BLOCK : (c + 1) * BLOCK, :] = chosen[:, c * 128 : (c + 1) * 128]
        for s in range(BLOCK):
            target = merged if s < FLIGHT else give
            f = s % FLIGHT
            value = tile[pl.ds(s, D // 128, stride=BLOCK), :].astype(BF16)
            target[stage, 2 * f] = value[0:16]
            target[stage, 2 * f + 1] = value[16:32]

    def give_pair(stage):
        send(give.at[stage], got.at[stage], pair_s.at[stage], pair_r.at[stage], x_pair)

    def all_z(stage, src, dst, send_sem, recv_sem):
        def body(i, carry):
            step = jnp.where(i % 2 == 1, (i + 1) // 2, Z - i // 2)
            zt = z_at(step)
            remote(src.at[zt], dst.at[z], send_sem, recv_sem, {"expert": zt * X + x}).start()
            return carry

        lax.fori_loop(1, Z, body, 0)
        dst[z] = src[z]
        sent.append(remote(src.at[pl.ds(0, Z - 1)], src.at[pl.ds(0, Z - 1)], send_sem, recv_sem, x_next))

    def merge(stage):
        arrived(got.at[stage], pair_r.at[stage])
        merged[stage] = merged[stage] + got[stage]
        all_z(stage, merged.at[stage], zin.at[stage], z_s.at[stage], z_r.at[stage])

    def place(stage, half, column, lo=0, width=HALF):
        start = pl.multiple_of((column + X) % X * BLOCK, BLOCK)
        return rows.at[stage, half, pl.ds(start, BLOCK), pl.ds(lo, width)]

    def hand(stage, ref, i, to):
        send(ref, ref, ag_s.at[stage, i], ag_r.at[stage, i], to)

    def take(stage, ref, i):
        arrived(ref, ag_r.at[stage, i])

    def gather(stage):
        arrived(zin.at[stage, pl.ds(0, Z - 1)], z_r.at[stage])
        for i in range(Z):
            tile2[pl.ds(i, 16, stride=Z), :] = zin[stage, i].astype(F32)
        mine = place(stage, h, x)
        for c in range(HALF // 128):
            mine[:, c * 128 : (c + 1) * 128] = tile2[c * BLOCK : (c + 1) * BLOCK, :].astype(BF16)
        hand(stage, mine, 0, z_pair)
        hand(stage, mine, 1, x_next)
        hand(stage, mine, 2, x_prev)

    def gather_far(stage):
        take(stage, place(stage, h, x - 1), 1)
        hand(stage, place(stage, h, x - 1, 0, MID), 5, x_next)
        take(stage, place(stage, h, x + 1), 2)
        hand(stage, place(stage, h, x + 1, MID, MID), 6, x_prev)

    def gather_twin(stage):
        twin = place(stage, 1 - h, x)
        take(stage, twin, 0)
        hand(stage, twin, 3, x_next)
        hand(stage, twin, 4, x_prev)

    def gather_cross(stage):
        for i in range(2):
            far = place(stage, h, x + 2, i * MID, MID)
            take(stage, far, 5 + i)
            hand(stage, far, 7 + i, z_pair)

    def gather_end(stage):
        take(stage, place(stage, 1 - h, x - 1), 3)
        take(stage, place(stage, 1 - h, x + 1), 4)
        for i in range(2):
            take(stage, place(stage, 1 - h, x + 2, i * MID, MID), 7 + i)

    select(0)
    select(1)
    pl.semaphore_wait(barrier, len(near))
    for step in (4, -4):
        greet(z_near, z_of(step))
    give_pair(0)
    give_pair(1)
    pl.semaphore_wait(z_near, 2)
    merge(0)
    merge(1)
    gather(0)
    gather(1)
    gather_far(0)
    gather_far(1)
    gather_twin(0)
    gather_twin(1)
    gather_cross(0)
    gather_cross(1)
    gather_end(0)
    for copy in loads[4:]:
        copy.wait()
    ab = dot(rows[0, 0], w[0:HALF, :]) + dot(rows[0, 1], w[HALF:D, :])
    gather_end(1)
    dh = lanes(rows[1, 0], wd[:, 0:HALF]) + lanes(rows[1, 1], wd[:, HALF:D])
    a, b = ab[:, 0:HD], ab[:, HD : 2 * HD]
    sig = 1.0 / (1.0 + jnp.exp(-a))
    act = a * sig
    grads = jnp.concatenate(
        (dh * b * sig * (1.0 + a * (1.0 - sig)), dh * act, act * b), axis=1
    )
    dab[...] = grads[:, 0 : 2 * HD].astype(BF16)
    gt[...] = jnp.transpose(grads).astype(BF16)

    def partial(far):
        yt = (y + far) % Y
        half = yt // 4
        cols = pl.ds(pl.multiple_of(yt % 4 * (2 * SLICE), 2 * SLICE), 2 * SLICE)
        gu = dot(gt[0 : 2 * HD, :], rows[0, half, :, cols])
        dn = dot(gt[2 * HD : GRADS, :], rows[1, half, :, cols])
        for c in range(2):
            part[far, c, 0 : 2 * HD, :] = gu[:, c * SLICE : (c + 1) * SLICE].astype(BF16)
            part[far, c, 2 * HD : GRADS, :] = dn[:, c * SLICE : (c + 1) * SLICE].astype(BF16)
        send(part.at[far, 1 - core], d2d.at[far], d2d_s.at[far], d2d_r.at[far], other_core)

    def both_cores(far):
        arrived(d2d.at[far], d2d_r.at[far])

    def own(far, piece):
        lo = piece * PIECE
        return part[far, core, lo : lo + PIECE, :].astype(F32) + d2d[far, lo : lo + PIECE, :].astype(F32)

    def ring(way, hops, piece):
        far = hops if way == 0 else Y - hops
        value = own(far, piece)
        if hops < 3 or (hops == 3 and piece // 2 == way):
            arrived(rin.at[way, hops, piece], ring_r.at[way, hops, piece])
            value = value + rin[way, hops, piece].astype(F32)
        rout[way, hops - 1, piece] = value.astype(BF16)
        send(
            rout.at[way, hops - 1, piece], rin.at[way, hops - 1, piece],
            ring_s.at[way, hops - 1, piece], ring_r.at[way, hops - 1, piece],
            y_next if way == 0 else y_prev,
        )

    def ring_step(hops, late):
        for i in range(2):
            for way in range(2):
                side = way if late else 1 - way
                ring(way, hops, 2 * side + i)

    def p_place(ref, column):
        start = pl.multiple_of((column + X) % X * BLOCK, BLOCK)
        return ref.at[pl.ds(start, BLOCK), :]

    p_order = (x + 2, x + 1, x - 1, x)

    def p_far():
        lo = pl.multiple_of((1 - h) * HALF, HALF)
        pz_out[...] = lanes(dab[...], w[pl.ds(lo, HALF), :]).astype(BF16)
        for i, column in enumerate(p_order):
            send(
                p_place(pz_out, column), p_place(pz_in, column), pz_s.at[i], pz_r.at[i], z_pair
            )

    def p_near():
        lo = pl.multiple_of(h * HALF, HALF)
        pm[...] = lanes(dab[...], w[pl.ds(lo, HALF), :])

    def p_sum(i):
        arrived(p_place(pz_in, p_order[i]), pz_r.at[i])
        return p_place(pm, p_order[i])[...] + p_place(pz_in, p_order[i])[...].astype(F32)

    def p_a():
        value = p_sum(0)
        for way in range(2):
            pa_out[way] = value[:, way * MID : (way + 1) * MID].astype(BF16)
            send(pa_out.at[way], pa_in.at[way], pa_s.at[way], pa_r.at[way], (x_next, x_prev)[way])

    def p_b():
        for way in range(2):
            value = p_sum(1 + way)
            for c in (1 - way, way):
                piece = value[:, c * MID : (c + 1) * MID]
                if c == way:
                    arrived(pa_in.at[way], pa_r.at[way])
                    piece = piece + pa_in[way].astype(F32)
                pb_out[way, c] = piece.astype(BF16)
                send(
                    pb_out.at[way, c], pb_in.at[way, c], pb_s.at[way, c], pb_r.at[way, c],
                    (x_next, x_prev)[way],
                )

    def p_back():
        mine = p_sum(3)
        for c in range(2):
            value = mine[:, c * MID : (c + 1) * MID]
            for way in (1 - c, c):
                arrived(pb_in.at[way, c], pb_r.at[way, c])
                value = value + pb_in[way, c].astype(F32)
            for i in range(MID // 128):
                lo = (c * (MID // 128) + i) * BLOCK
                tile2[lo : lo + BLOCK, :] = value[:, i * 128 : (i + 1) * 128]
        for i in range(Z):
            zq_out[i] = tile2[pl.ds(i, 16, stride=Z), :].astype(BF16)
        all_z(0, zq_out, zq_in, zq_sem.at[0], zq_sem.at[1])

    def p_pair():
        arrived(zq_in.at[pl.ds(0, Z - 1)], zq_sem.at[1])
        send(zq_in, pq_in, pq_sem.at[0], pq_sem.at[1], x_pair)

    def p_tokens():
        for f in range(FLIGHT):
            for half in range(2):
                tile[pl.ds(half * 256 + f, 16, stride=BLOCK), :] = zq_in[2 * f + half].astype(F32)
        arrived(pq_in, pq_sem.at[1])
        for f in range(FLIGHT):
            for half in range(2):
                tile[pl.ds(half * 256 + FLIGHT + f, 16, stride=BLOCK), :] = pq_in[2 * f + half].astype(F32)
        for c in range(D // 128):
            prow[:, c * 128 : (c + 1) * 128] = tile[c * BLOCK : (c + 1) * BLOCK, :].astype(BF16)

    partial(4)
    p_far()
    partial(3)
    partial(5)
    both_cores(4)
    for i in range(2):
        ring(0, 4, i)
        ring(1, 4, 2 + i)
    both_cores(3)
    both_cores(5)
    ring_step(3, False)
    p_near()
    partial(2)
    partial(6)
    p_a()
    partial(1)
    partial(7)
    partial(0)
    ring_step(3, True)
    p_b()
    both_cores(2)
    both_cores(6)
    ring_step(2, False)
    p_back()
    ring_step(2, True)
    both_cores(1)
    both_cores(7)
    ring_step(1, False)
    ring_step(1, True)
    p_pair()
    both_cores(0)
    for piece in range(PIECES):
        value = own(0, piece)
        for way in range(2):
            arrived(rin.at[way, 0, piece], ring_r.at[way, 0, piece])
            value = value + rin[way, 0, piece].astype(F32)
        total_out[piece * PIECE : (piece + 1) * PIECE, :] = value
    p_tokens()
    for copy in sent:
        copy.wait_send()


def finish(prow, pick_t, total, tg_hbm, gg_hbm, ug_hbm, dg_hbm, tg, gg, ug, dg, sems):
    copies = []

    def out(src, dst):
        copies.append(pltpu.make_async_copy(src, dst, sems.at[len(copies)]))
        copies[-1].start()

    for c in range(4):
        cols = slice(c * (D // 4), (c + 1) * (D // 4))
        tg[:, cols] = dot(pick_t[...], prow[:, cols]).astype(BF16)
        out(tg.at[:, cols], tg_hbm.at[:, cols])
    dg[...] = total[2 * HD : GRADS, :].astype(BF16)
    out(dg, dg_hbm)
    gg[...] = jnp.transpose(total[0:HD, :]).astype(BF16)
    out(gg, gg_hbm)
    ug[...] = jnp.transpose(total[HD : 2 * HD, :]).astype(BF16)
    out(ug, ug_hbm)
    for copy in copies:
        copy.wait()


def shards(tokens, cotangent, slot_token, slot_gate, gate_weight, up_weight, down_weight):
    hbm = pl.BlockSpec(memory_space=pltpu.HBM)
    vmem = pl.BlockSpec(memory_space=pltpu.VMEM)
    dma = pltpu.SemaphoreType.DMA
    prow, pick_t, total = pl.pallas_call(
        kernel,
        out_shape=(
            pltpu.VMEM((BLOCK, D), BF16),
            pltpu.VMEM((TOK, BLOCK), BF16),
            pltpu.VMEM((GRADS, SLICE), F32),
        ),
        in_specs=[hbm] * 7,
        out_specs=(vmem,) * 3,
        scratch_shapes=[
            pltpu.SMEM((1, 2 * FLIGHT), jnp.int32),
            pltpu.SMEM((1, 2 * FLIGHT), jnp.int32),
            pltpu.VMEM((TOK, D), BF16),
            pltpu.VMEM((TOK, D), BF16),
            pltpu.VMEM((D, 2 * HD), BF16),
            pltpu.VMEM((HD, D), BF16),
            pltpu.VMEM((D // 128 * BLOCK, 128), F32),
            pltpu.VMEM((HALF // 128 * BLOCK, 128), F32),
            pltpu.VMEM((2, Z, 16, 128), BF16),
            pltpu.VMEM((2, Z, 16, 128), BF16),
            pltpu.VMEM((2, Z, 16, 128), BF16),
            pltpu.VMEM((2, Z, 16, 128), BF16),
            pltpu.VMEM((2, 2, ROWS, HALF), BF16),
            pltpu.VMEM((ROWS, 2 * HD), BF16),
            pltpu.VMEM((GRADS, ROWS), BF16),
            pltpu.VMEM((Y, 2, GRADS, SLICE), BF16),
            pltpu.VMEM((Y, GRADS, SLICE), BF16),
            pltpu.VMEM((2, 4, PIECES, PIECE, SLICE), BF16),
            pltpu.VMEM((2, 4, PIECES, PIECE, SLICE), BF16),
            pltpu.VMEM((ROWS, HALF), BF16),
            pltpu.VMEM((ROWS, HALF), BF16),
            pltpu.VMEM((ROWS, HALF), F32),
            pltpu.VMEM((2, BLOCK, MID), BF16),
            pltpu.VMEM((2, BLOCK, MID), BF16),
            pltpu.VMEM((2, 2, BLOCK, MID), BF16),
            pltpu.VMEM((2, 2, BLOCK, MID), BF16),
            pltpu.VMEM((Z, 16, 128), BF16),
            pltpu.VMEM((Z, 16, 128), BF16),
            pltpu.VMEM((Z, 16, 128), BF16),
            dma((7,)),
            dma((2,)),
            dma((2,)),
            dma((2,)),
            dma((2,)),
            dma((2, 9)),
            dma((2, 9)),
            dma((Y,)),
            dma((Y,)),
            dma((2, 4, PIECES)),
            dma((2, 4, PIECES)),
            dma((4,)),
            dma((4,)),
            dma((2,)),
            dma((2,)),
            dma((2, 2)),
            dma((2, 2)),
            dma((2,)),
            dma((2,)),
            pltpu.SemaphoreType.REGULAR,
        ],
        compiler_params=pltpu.CompilerParams(
            collective_id=0, has_side_effects=True, vmem_limit_bytes=60 * 1024 * 1024
        ),
        name="moe_backward",
    )(slot_token, slot_gate, tokens, cotangent, gate_weight, up_weight, down_weight)

    shapes = ((TOK, D), (SLICE, HD), (SLICE, HD), (HD, SLICE))
    return pl.pallas_call(
        finish,
        out_shape=tuple(jax.ShapeDtypeStruct(shape, BF16) for shape in shapes),
        in_specs=[vmem] * 3,
        out_specs=(hbm,) * 4,
        scratch_shapes=[pltpu.VMEM(shape, BF16) for shape in shapes] + [dma((7,))],
        compiler_params=pltpu.CompilerParams(vmem_limit_bytes=32 * 1024 * 1024),
        name="finish",
    )(prow, pick_t, total)


def solution(mesh):
    placed = (
        P(("dp", "expert"), None),
        P(("dp", "expert"), None),
        P(("dp", "expert"), None),
        P(("dp", "expert"), None),
        P(None, "expert"),
        P(None, "expert"),
        P("expert", None),
    )
    return jax.shard_map(
        shards,
        mesh=mesh,
        in_specs=placed,
        out_specs=(
            P(("dp", "expert"), None),
            P("dp", "expert"),
            P("dp", "expert"),
            P("expert", "dp"),
        ),
        check_vma=False,
    )
```

```python
import jax
import jax.numpy as jnp
from jax import lax
from jax.experimental import pallas as pl
from jax.experimental.pallas import tpu as pltpu
from jax.sharding import PartitionSpec as P

F32 = jnp.float32
BF16 = jnp.bfloat16
MESH = pl.DeviceIdType.MESH

X = 4
Y = 8
Z = 16
D = 4096
HALF = D // 2
FLIGHT = 8
TOK = 128
HD = 128
BLOCK = 16
ROWS = BLOCK * X
SLICE = 256
GRADS = 3 * HD
PIECES = 4
PIECE = GRADS // PIECES
MID = HALF // 2


def lanes(a, b):
    return lax.dot_general(a, b, (((1,), (1,)), ((), ())), preferred_element_type=F32)


def dot(a, b):
    return jnp.dot(a, b, preferred_element_type=F32)


def kernel(
    st_hbm, sg_hbm, tok_hbm, cot_hbm, wg_hbm, wu_hbm, wd_hbm,
    prow, pick_out, total_out,
    st, sg, tok, cot, w, wd, tile, tile2, merged, give, got, zin, rows, dab, gt,
    part, d2d, rout, rin, pz_out, pz_in, pm, pa_out, pa_in, pb_out, pb_in,
    zq_out, zq_in, pq_in,
    load_sem, pair_s, pair_r, z_s, z_r, ag_s, ag_r, d2d_s, d2d_r, ring_s, ring_r,
    pz_s, pz_r, pa_s, pa_r, pb_s, pb_r, zq_sem, pq_sem, z_near,
):
    d = lax.axis_index("dp")
    e = lax.axis_index("expert")
    y, core = d // 2, d % 2
    z, x = e // X, e % X
    h = z % 2
    other_core = {"dp": y * 2 + 1 - core}
    y_next = {"dp": (y + 1) % Y * 2 + core}
    y_prev = {"dp": (y + Y - 1) % Y * 2 + core}
    x_next = {"expert": z * X + (x + 1) % X}
    x_prev = {"expert": z * X + (x + X - 1) % X}
    x_pair = {"expert": e + 1 - 2 * (x % 2)}
    z_pair = {"expert": e + X - 2 * X * h}

    places = ((2, 1), (2, 0), (1, 1), (-1, 1), (0, 1), (1, 0), (-1, 0))

    def mate(across, over):
        column = (x + across + X) % X
        return {"expert": (z + over * (1 - 2 * h)) * X + column}

    def remote(src, dst, send_sem, recv_sem, to):
        return pltpu.make_async_remote_copy(
            src_ref=src, dst_ref=dst, send_sem=send_sem, recv_sem=recv_sem,
            device_id=to, device_id_type=MESH,
        )

    sent = []

    def send(src, dst, send_sem, recv_sem, to):
        copy = remote(src, dst, send_sem, recv_sem, to)
        copy.start()
        sent.append(copy)

    def arrived(dst, recv_sem):
        remote(dst, dst, recv_sem, recv_sem, other_core).wait_recv()

    barrier = pltpu.get_barrier_semaphore()

    def z_at(i):
        return (z + i) % Z

    def z_of(step):
        return {"expert": z_at(step + Z) * X + x}

    def greet(semaphore, to):
        pl.semaphore_signal(semaphore, inc=1, device_id=to, device_id_type=MESH)

    near = [z_of(way * step) for step in (4, 3, 2, 1) for way in (1, -1)]
    near += [x_next, x_prev, other_core, y_next, y_prev]
    near += [mate(across, over) for across, over in places if across == 2 or over and across]
    for to in near:
        greet(barrier, to)

    loads = [
        pltpu.make_async_copy(src, dst, load_sem.at[i])
        for i, (src, dst) in enumerate(
            (
                (st_hbm, st),
                (sg_hbm, sg),
                (tok_hbm, tok),
                (cot_hbm, cot),
                (wg_hbm, w.at[:, 0:HD]),
                (wu_hbm, w.at[:, HD : 2 * HD]),
                (wd_hbm, wd),
            )
        )
    ]
    for copy in loads:
        copy.start()

    loads[0].wait()
    loads[1].wait()

    line = lax.broadcasted_iota(jnp.int32, (BLOCK, TOK), 0)
    lane = lax.broadcasted_iota(jnp.int32, (BLOCK, TOK), 1)
    row_t = lax.broadcasted_iota(jnp.int32, (TOK, BLOCK), 0)
    col_t = lax.broadcasted_iota(jnp.int32, (TOK, BLOCK), 1)
    pick = jnp.zeros((BLOCK, TOK), F32)
    pick_t = jnp.zeros((TOK, BLOCK), F32)
    weight = jnp.zeros((BLOCK, TOK), F32)
    for k in range(2):
        for f in range(FLIGHT):
            s = k * FLIGHT + f
            code = sg[0, f * 2 + k]
            token = jnp.where(code != 0, st[0, f * 2 + k], -1)
            pick = jnp.where((line == s) & (lane == token), 1.0, pick)
            pick_t = jnp.where((col_t == s) & (row_t == token), 1.0, pick_t)
            weight = jnp.where(line == s, code.astype(F32) / 1024.0, weight)
    pick = pick.astype(BF16)
    pick_out[...] = pick_t.astype(BF16)

    def select(stage):
        source = (tok, cot)[stage]
        loads[2 + stage].wait()
        chosen = dot(pick, source[...])
        if stage == 1:
            chosen = chosen * weight[:, 0:1]
        for c in range(D // 128):
            tile[c * BLOCK : (c + 1) * BLOCK, :] = chosen[:, c * 128 : (c + 1) * 128]
        for s in range(BLOCK):
            target = merged if s < FLIGHT else give
            f = s % FLIGHT
            value = tile[pl.ds(s, D // 128, stride=BLOCK), :].astype(BF16)
            target[stage, 2 * f] = value[0:16]
            target[stage, 2 * f + 1] = value[16:32]

    def give_pair(stage):
        send(give.at[stage], got.at[stage], pair_s.at[stage], pair_r.at[stage], x_pair)

    def all_z(stage, src, dst, send_sem, recv_sem):
        def body(i, carry):
            step = jnp.where(i % 2 == 1, (i + 1) // 2, Z - i // 2)
            zt = z_at(step)
            remote(src.at[zt], dst.at[z], send_sem, recv_sem, {"expert": zt * X + x}).start()
            return carry

        lax.fori_loop(1, Z, body, 0)
        dst[z] = src[z]
        sent.append(remote(src.at[pl.ds(0, Z - 1)], src.at[pl.ds(0, Z - 1)], send_sem, recv_sem, x_next))

    def merge(stage):
        arrived(got.at[stage], pair_r.at[stage])
        merged[stage] = merged[stage] + got[stage]
        all_z(stage, merged.at[stage], zin.at[stage], z_s.at[stage], z_r.at[stage])

    def place(stage, half, column, lo=0, width=HALF):
        start = pl.multiple_of((column + X) % X * BLOCK, BLOCK)
        return rows.at[stage, half, pl.ds(start, BLOCK), pl.ds(lo, width)]

    def hand(stage, ref, i, to):
        send(ref, ref, ag_s.at[stage, i], ag_r.at[stage, i], to)

    def take(stage, ref, i):
        arrived(ref, ag_r.at[stage, i])

    def gather(stage):
        arrived(zin.at[stage, pl.ds(0, Z - 1)], z_r.at[stage])
        for i in range(Z):
            tile2[pl.ds(i, 16, stride=Z), :] = zin[stage, i].astype(F32)
        mine = place(stage, h, x)
        for c in range(HALF // 128):
            mine[:, c * 128 : (c + 1) * 128] = tile2[c * BLOCK : (c + 1) * BLOCK, :].astype(BF16)
        for i, (across, over) in enumerate(places):
            hand(stage, mine, i, mate(across, over))

    def gather_end(stage):
        for i, (across, over) in enumerate(places):
            take(stage, place(stage, 1 - h if over else h, x - across), i)

    select(0)
    select(1)
    pl.semaphore_wait(barrier, len(near))
    for step in (4, -4):
        greet(z_near, z_of(step))
    give_pair(0)
    give_pair(1)
    pl.semaphore_wait(z_near, 2)
    merge(0)
    merge(1)
    gather(0)
    gather(1)
    gather_end(0)
    for copy in loads[4:]:
        copy.wait()
    ab = dot(rows[0, 0], w[0:HALF, :]) + dot(rows[0, 1], w[HALF:D, :])
    gather_end(1)
    dh = lanes(rows[1, 0], wd[:, 0:HALF]) + lanes(rows[1, 1], wd[:, HALF:D])
    a, b = ab[:, 0:HD], ab[:, HD : 2 * HD]
    sig = 1.0 / (1.0 + jnp.exp(-a))
    act = a * sig
    grads = jnp.concatenate(
        (dh * b * sig * (1.0 + a * (1.0 - sig)), dh * act, act * b), axis=1
    )
    dab[...] = grads[:, 0 : 2 * HD].astype(BF16)
    gt[...] = jnp.transpose(grads).astype(BF16)

    def partial(far):
        yt = (y + far) % Y
        half = yt // 4
        cols = pl.ds(pl.multiple_of(yt % 4 * (2 * SLICE), 2 * SLICE), 2 * SLICE)
        gu = dot(gt[0 : 2 * HD, :], rows[0, half, :, cols])
        dn = dot(gt[2 * HD : GRADS, :], rows[1, half, :, cols])
        for c in range(2):
            part[far, c, 0 : 2 * HD, :] = gu[:, c * SLICE : (c + 1) * SLICE].astype(BF16)
            part[far, c, 2 * HD : GRADS, :] = dn[:, c * SLICE : (c + 1) * SLICE].astype(BF16)
        send(part.at[far, 1 - core], d2d.at[far], d2d_s.at[far], d2d_r.at[far], other_core)

    def both_cores(far):
        arrived(d2d.at[far], d2d_r.at[far])

    def own(far, piece):
        lo = piece * PIECE
        return part[far, core, lo : lo + PIECE, :].astype(F32) + d2d[far, lo : lo + PIECE, :].astype(F32)

    def ring(way, hops, piece):
        far = hops if way == 0 else Y - hops
        value = own(far, piece)
        if hops < 3 or (hops == 3 and piece // 2 == way):
            arrived(rin.at[way, hops, piece], ring_r.at[way, hops, piece])
            value = value + rin[way, hops, piece].astype(F32)
        rout[way, hops - 1, piece] = value.astype(BF16)
        send(
            rout.at[way, hops - 1, piece], rin.at[way, hops - 1, piece],
            ring_s.at[way, hops - 1, piece], ring_r.at[way, hops - 1, piece],
            y_next if way == 0 else y_prev,
        )

    def ring_step(hops, late):
        for i in range(2):
            for way in range(2):
                side = way if late else 1 - way
                ring(way, hops, 2 * side + i)

    def p_place(ref, column):
        start = pl.multiple_of((column + X) % X * BLOCK, BLOCK)
        return ref.at[pl.ds(start, BLOCK), :]

    p_order = (x + 2, x + 1, x - 1, x)

    def p_far():
        lo = pl.multiple_of((1 - h) * HALF, HALF)
        pz_out[...] = lanes(dab[...], w[pl.ds(lo, HALF), :]).astype(BF16)
        for i, column in enumerate(p_order):
            send(
                p_place(pz_out, column), p_place(pz_in, column), pz_s.at[i], pz_r.at[i], z_pair
            )

    def p_near():
        lo = pl.multiple_of(h * HALF, HALF)
        pm[...] = lanes(dab[...], w[pl.ds(lo, HALF), :])

    def p_sum(i):
        arrived(p_place(pz_in, p_order[i]), pz_r.at[i])
        return p_place(pm, p_order[i])[...] + p_place(pz_in, p_order[i])[...].astype(F32)

    def p_a():
        value = p_sum(0)
        for way in range(2):
            pa_out[way] = value[:, way * MID : (way + 1) * MID].astype(BF16)
            send(pa_out.at[way], pa_in.at[way], pa_s.at[way], pa_r.at[way], (x_next, x_prev)[way])

    def p_b():
        for way in range(2):
            value = p_sum(1 + way)
            for c in (1 - way, way):
                piece = value[:, c * MID : (c + 1) * MID]
                if c == way:
                    arrived(pa_in.at[way], pa_r.at[way])
                    piece = piece + pa_in[way].astype(F32)
                pb_out[way, c] = piece.astype(BF16)
                send(
                    pb_out.at[way, c], pb_in.at[way, c], pb_s.at[way, c], pb_r.at[way, c],
                    (x_next, x_prev)[way],
                )

    def p_back():
        mine = p_sum(3)
        for c in range(2):
            value = mine[:, c * MID : (c + 1) * MID]
            for way in (1 - c, c):
                arrived(pb_in.at[way, c], pb_r.at[way, c])
                value = value + pb_in[way, c].astype(F32)
            for i in range(MID // 128):
                lo = (c * (MID // 128) + i) * BLOCK
                tile2[lo : lo + BLOCK, :] = value[:, i * 128 : (i + 1) * 128]
        for i in range(Z):
            zq_out[i] = tile2[pl.ds(i, 16, stride=Z), :].astype(BF16)
        all_z(0, zq_out, zq_in, zq_sem.at[0], zq_sem.at[1])

    def p_pair():
        arrived(zq_in.at[pl.ds(0, Z - 1)], zq_sem.at[1])
        send(zq_in, pq_in, pq_sem.at[0], pq_sem.at[1], x_pair)

    def p_tokens():
        for f in range(FLIGHT):
            for half in range(2):
                tile[pl.ds(half * 256 + f, 16, stride=BLOCK), :] = zq_in[2 * f + half].astype(F32)
        arrived(pq_in, pq_sem.at[1])
        for f in range(FLIGHT):
            for half in range(2):
                tile[pl.ds(half * 256 + FLIGHT + f, 16, stride=BLOCK), :] = pq_in[2 * f + half].astype(F32)
        for c in range(D // 128):
            prow[:, c * 128 : (c + 1) * 128] = tile[c * BLOCK : (c + 1) * BLOCK, :].astype(BF16)

    partial(4)
    p_far()
    partial(3)
    partial(5)
    both_cores(4)
    for i in range(2):
        ring(0, 4, i)
        ring(1, 4, 2 + i)
    both_cores(3)
    both_cores(5)
    ring_step(3, False)
    p_near()
    partial(2)
    partial(6)
    p_a()
    partial(1)
    partial(7)
    partial(0)
    ring_step(3, True)
    p_b()
    both_cores(2)
    both_cores(6)
    ring_step(2, False)
    p_back()
    ring_step(2, True)
    both_cores(1)
    both_cores(7)
    ring_step(1, False)
    ring_step(1, True)
    p_pair()
    both_cores(0)
    for piece in range(PIECES):
        value = own(0, piece)
        for way in range(2):
            arrived(rin.at[way, 0, piece], ring_r.at[way, 0, piece])
            value = value + rin[way, 0, piece].astype(F32)
        total_out[piece * PIECE : (piece + 1) * PIECE, :] = value
    p_tokens()
    for copy in sent:
        copy.wait_send()


def finish(prow, pick_t, total, tg_hbm, gg_hbm, ug_hbm, dg_hbm, tg, gg, ug, dg, sems):
    copies = []

    def out(src, dst):
        copies.append(pltpu.make_async_copy(src, dst, sems.at[len(copies)]))
        copies[-1].start()

    for c in range(4):
        cols = slice(c * (D // 4), (c + 1) * (D // 4))
        tg[:, cols] = dot(pick_t[...], prow[:, cols]).astype(BF16)
        out(tg.at[:, cols], tg_hbm.at[:, cols])
    dg[...] = total[2 * HD : GRADS, :].astype(BF16)
    out(dg, dg_hbm)
    gg[...] = jnp.transpose(total[0:HD, :]).astype(BF16)
    out(gg, gg_hbm)
    ug[...] = jnp.transpose(total[HD : 2 * HD, :]).astype(BF16)
    out(ug, ug_hbm)
    for copy in copies:
        copy.wait()


def shards(tokens, cotangent, slot_token, slot_gate, gate_weight, up_weight, down_weight):
    hbm = pl.BlockSpec(memory_space=pltpu.HBM)
    vmem = pl.BlockSpec(memory_space=pltpu.VMEM)
    dma = pltpu.SemaphoreType.DMA
    prow, pick_t, total = pl.pallas_call(
        kernel,
        out_shape=(
            pltpu.VMEM((BLOCK, D), BF16),
            pltpu.VMEM((TOK, BLOCK), BF16),
            pltpu.VMEM((GRADS, SLICE), F32),
        ),
        in_specs=[hbm] * 7,
        out_specs=(vmem,) * 3,
        scratch_shapes=[
            pltpu.SMEM((1, 2 * FLIGHT), jnp.int32),
            pltpu.SMEM((1, 2 * FLIGHT), jnp.int32),
            pltpu.VMEM((TOK, D), BF16),
            pltpu.VMEM((TOK, D), BF16),
            pltpu.VMEM((D, 2 * HD), BF16),
            pltpu.VMEM((HD, D), BF16),
            pltpu.VMEM((D // 128 * BLOCK, 128), F32),
            pltpu.VMEM((HALF // 128 * BLOCK, 128), F32),
            pltpu.VMEM((2, Z, 16, 128), BF16),
            pltpu.VMEM((2, Z, 16, 128), BF16),
            pltpu.VMEM((2, Z, 16, 128), BF16),
            pltpu.VMEM((2, Z, 16, 128), BF16),
            pltpu.VMEM((2, 2, ROWS, HALF), BF16),
            pltpu.VMEM((ROWS, 2 * HD), BF16),
            pltpu.VMEM((GRADS, ROWS), BF16),
            pltpu.VMEM((Y, 2, GRADS, SLICE), BF16),
            pltpu.VMEM((Y, GRADS, SLICE), BF16),
            pltpu.VMEM((2, 4, PIECES, PIECE, SLICE), BF16),
            pltpu.VMEM((2, 4, PIECES, PIECE, SLICE), BF16),
            pltpu.VMEM((ROWS, HALF), BF16),
            pltpu.VMEM((ROWS, HALF), BF16),
            pltpu.VMEM((ROWS, HALF), F32),
            pltpu.VMEM((2, BLOCK, MID), BF16),
            pltpu.VMEM((2, BLOCK, MID), BF16),
            pltpu.VMEM((2, 2, BLOCK, MID), BF16),
            pltpu.VMEM((2, 2, BLOCK, MID), BF16),
            pltpu.VMEM((Z, 16, 128), BF16),
            pltpu.VMEM((Z, 16, 128), BF16),
            pltpu.VMEM((Z, 16, 128), BF16),
            dma((7,)),
            dma((2,)),
            dma((2,)),
            dma((2,)),
            dma((2,)),
            dma((2, 7)),
            dma((2, 7)),
            dma((Y,)),
            dma((Y,)),
            dma((2, 4, PIECES)),
            dma((2, 4, PIECES)),
            dma((4,)),
            dma((4,)),
            dma((2,)),
            dma((2,)),
            dma((2, 2)),
            dma((2, 2)),
            dma((2,)),
            dma((2,)),
            pltpu.SemaphoreType.REGULAR,
        ],
        compiler_params=pltpu.CompilerParams(
            collective_id=0, has_side_effects=True, vmem_limit_bytes=60 * 1024 * 1024
        ),
        name="moe_backward",
    )(slot_token, slot_gate, tokens, cotangent, gate_weight, up_weight, down_weight)

    shapes = ((TOK, D), (SLICE, HD), (SLICE, HD), (HD, SLICE))
    return pl.pallas_call(
        finish,
        out_shape=tuple(jax.ShapeDtypeStruct(shape, BF16) for shape in shapes),
        in_specs=[vmem] * 3,
        out_specs=(hbm,) * 4,
        scratch_shapes=[pltpu.VMEM(shape, BF16) for shape in shapes] + [dma((7,))],
        compiler_params=pltpu.CompilerParams(vmem_limit_bytes=32 * 1024 * 1024),
        name="finish",
    )(prow, pick_t, total)


def solution(mesh):
    placed = (
        P(("dp", "expert"), None),
        P(("dp", "expert"), None),
        P(("dp", "expert"), None),
        P(("dp", "expert"), None),
        P(None, "expert"),
        P(None, "expert"),
        P("expert", None),
    )
    return jax.shard_map(
        shards,
        mesh=mesh,
        in_specs=placed,
        out_specs=(
            P(("dp", "expert"), None),
            P("dp", "expert"),
            P("dp", "expert"),
            P("expert", "dp"),
        ),
        check_vma=False,
    )
```
